32 devices in a mesh: tm: 8 (over z, y), panel: 4 (over x, core).
Axes of the slice: x: 2, y: 2, z: 4, core: 2. Of those that a mesh axis runs over, the one named last changes fastest.
Arguments:
- record: bfloat16 [16384, 1024], P('tm'), may hold values from -6 to 6
- eigvecs: bfloat16 [16384, 32], P(('tm', 'panel')), may hold values from -2.5 to 2.5
- starts: int32 [8], P('panel'), may hold values from 0 to 15616, as said below
- kernel_width: float32 [1], replicated, may hold values from 0.025 to 0.1
Outputs:
- applied: float32 [8, 768, 32], P('panel', 'tm')
The draws below stay inside these ranges and needn't reach their ends.
Inputs may be any that keep to these rules, and one draw needn't show every extreme that they name: Some panel starts at 0 and some at 15616.
All inputs are finite; a program needn't handle non-finite values.
Results may differ from the reference program's by a relative error of at most 0.0003.
Values may be sent and summed in bfloat16 or wider, within the bound.
No kernel may reach another device: no remote copies, remote signals or barrier semaphores. Data moves between devices by JAX's collectives and lax.ppermute only.
A program may use at most 128 MiB of HBM per device.

```python
import math
import jax
import jax.numpy as jnp
from jax import lax

CHANNELS = 1024
DELAYS = 64
PANEL = 768
MODES = 32
SAMPLE_TOTAL = 16384
PANELS = 8


def oscillator_angles(key):
    subkeys = jax.random.split(key, 4)
    sample_position = jnp.arange(SAMPLE_TOTAL, dtype=jnp.float32)
    period_number = jax.random.uniform(subkeys[0], (3,), jnp.float32, 20.0, 60.0)
    wobble_cycles = jax.random.uniform(subkeys[1], (3,), jnp.float32, 1.5, 3.5)
    swing_depth = jax.random.uniform(subkeys[2], (3,), jnp.float32, 1.5, 2.5)
    angular_shifts = jax.random.uniform(subkeys[3], (2, 3), jnp.float32, 0.0, 2.0 * math.pi)
    base_sinusoid = jnp.mod(sample_position[:, None] * (period_number / SAMPLE_TOTAL)[None, :], 1.0)
    wobble = jnp.mod(sample_position[:, None] * (wobble_cycles / SAMPLE_TOTAL)[None, :], 1.0)
    oscillation_height = swing_depth[None, :] * jnp.sin(2.0 * math.pi * wobble + angular_shifts[1][None, :])
    return 2.0 * math.pi * base_sinusoid + angular_shifts[0][None, :] + oscillation_height


def draw_record(key, part):
    angles = oscillator_angles(key)
    key = jax.random.fold_in(key, 11)
    subkeys = jax.random.split(key, 7)
    lead_count = max(CHANNELS // 16, 6)
    weak_count = CHANNELS - lead_count
    lead_group = jnp.arange(lead_count, dtype=jnp.int32) % 3
    forcing_strength = jnp.exp(jax.random.uniform(subkeys[0], (3,), jnp.float32, math.log(0.1), math.log(0.2)))
    lead_scale = jnp.exp(jax.random.uniform(subkeys[1], (lead_count,), jnp.float32, math.log(0.7), math.log(1.4)))
    weak_amps = jnp.exp(jax.random.uniform(subkeys[4], (weak_count,), jnp.float32, math.log(0.05), math.log(0.5)))
    noise_part = 0.12 * jax.random.truncated_normal(subkeys[5], -3.0, 3.0, (SAMPLE_TOTAL, CHANNELS), jnp.float32)
    lead_amps = jnp.sqrt(CHANNELS * 3.0 * forcing_strength[lead_group] / lead_count) * lead_scale
    lead_offsets = jax.random.uniform(subkeys[2], (lead_count,), jnp.float32, 0.0, 2.0 * math.pi)
    leading = lead_amps[None, :] * jnp.sin(jnp.take(angles, lead_group, axis=1) + lead_offsets[None, :])
    weak_rates = jnp.exp(jax.random.uniform(subkeys[3], (weak_count,), jnp.float32, math.log(1.0 / 2000.0), math.log(1.0 / 16.0)))
    weak_offsets = jax.random.uniform(subkeys[6], (weak_count,), jnp.float32, 0.0, 2.0 * math.pi)
    sample_position = jnp.arange(SAMPLE_TOTAL, dtype=jnp.float32)
    weak_turns = jnp.mod(sample_position[:, None] * weak_rates[None, :], 1.0)
    weak_part = weak_amps[None, :] * jnp.sin(2.0 * math.pi * weak_turns + weak_offsets[None, :])
    return (jnp.concatenate([leading, weak_part], axis=1) + noise_part).astype(jnp.bfloat16)


def draw_eigvecs(key, part):
    angles = oscillator_angles(key)
    key = jax.random.fold_in(key, 29)
    subkeys = jax.random.split(key, 2)
    mode_index = jnp.arange(MODES, dtype=jnp.int32)
    which_osc = mode_index % 3
    harmonic = (1 + mode_index // 3 % 2).astype(jnp.float32)
    offsets = jax.random.uniform(subkeys[0], (MODES,), jnp.float32, 0.0, 2.0 * math.pi)
    smooth = jnp.cos(jnp.take(angles, which_osc, axis=1) * harmonic[None, :] + offsets[None, :])
    values = smooth + 0.5 * jax.random.truncated_normal(subkeys[1], -3.0, 3.0, (SAMPLE_TOTAL, MODES), jnp.float32)
    return values.astype(jnp.bfloat16)


def draw_starts(key, part):
    key = jax.random.fold_in(key, 23)
    subkeys = jax.random.split(key, 2)
    values = jax.random.randint(subkeys[0], (PANELS,), 0, SAMPLE_TOTAL - PANEL + 1)
    order = jax.random.permutation(subkeys[1], PANELS)
    values = values.at[order[0]].set(0)
    values = values.at[order[1]].set(SAMPLE_TOTAL - PANEL)
    return values.astype(jnp.int32)


def setup_inputs(seed: int = 0) -> dict:
    streams_of = jax.random.split(jax.random.key(seed), 5)
    record = draw_record(jax.random.fold_in(streams_of[4], 71), 0)
    eigvecs = draw_eigvecs(jax.random.fold_in(streams_of[4], 71), 0)
    starts = draw_starts(jax.random.fold_in(streams_of[4], 71), 0)
    kernel_width = jnp.clip(jnp.exp(jax.random.uniform(streams_of[3], (1,), jnp.float32, math.log(0.025), math.log(0.1))), 0.025, 0.1)
    return {"record": record, "eigvecs": eigvecs, "starts": starts, "kernel_width": kernel_width}


def lag_sums(summed):
    stride = 1
    while stride < DELAYS:
        if summed.ndim == 2:
            summed = summed[:-stride, :-stride] + summed[stride:, stride:]
        else:
            summed = summed[:-stride] + summed[stride:]
        stride = stride * 2
    return summed


def reference(record, eigvecs, starts, kernel_width):
    record_length = PANEL + DELAYS - 1
    padded = jnp.concatenate([jnp.zeros((DELAYS - 1, CHANNELS), jnp.bfloat16), record], axis=0)
    energy = jnp.sum(jnp.square(padded.astype(jnp.float32)), axis=1)
    column_norms = lag_sums(energy)
    spread = kernel_width[0] * (DELAYS * CHANNELS)
    results = []
    for number in range(PANELS):
        window = lax.dynamic_slice_in_dim(padded, starts[number].astype(jnp.int32), record_length, 0)
        row_norms = lag_sums(jnp.sum(jnp.square(window.astype(jnp.float32)), axis=1))
        gram = lax.dot_general(window, padded, (((1,), (1,)), ((), ())), preferred_element_type=jnp.float32)
        inner = lag_sums(gram)
        distance = row_norms[:, None] + column_norms[None, :] - 2.0 * inner
        kernel = jnp.exp(-distance / spread)
        total = jnp.sum(kernel, axis=1)
        numer = jnp.dot(kernel.astype(jnp.bfloat16), eigvecs, preferred_element_type=jnp.float32)
        results.append(numer / total[:, None])
    return jnp.stack(results)
```

```python
import jax
import jax.numpy as jnp
from jax import lax
from jax.experimental import pallas as pl
from jax.experimental.pallas import tpu as pltpu
from jax.sharding import PartitionSpec as P

DELAYS = 64
PANEL = 768
SLOTS = 2
GROUP = 16
LANES = 128
MODES = 32
BIG = 1e30


def panel_kernel(homes, parts, meta, scale, record, rim, vectors, norms, *rest):
    shards = rest[:parts]
    out, window, turned, gram, strips, weights, sums, result = rest[parts:]
    columns = record.shape[0]
    width = columns + LANES
    tiles = width // LANES
    rows = window.shape[0]
    used = turned.shape[0]
    kept = used - DELAYS
    modes = MODES
    for number in range(parts):
        first = meta[number]
        for step in range(shards[number].shape[0]):
            place = pl.multiple_of((first + homes * step) * GROUP, GROUP)
            window[pl.ds(place, GROUP), :] = shards[number][step]
    low = 0
    while low < used:
        count = min(LANES, used - low)
        turn = lax.broadcasted_iota(jnp.int32, (count, count), 0) + lax.broadcasted_iota(jnp.int32, (count, count), 1)
        flip = jnp.where(turn == count - 1, 2.0, 0.0).astype(jnp.bfloat16)
        block = jnp.dot(flip, window[used - low - count : used - low, :], preferred_element_type=jnp.float32)
        turned[low : low + count, :] = block.astype(jnp.bfloat16)
        energy = jnp.sum(block * block, axis=1, keepdims=True) * 0.25
        strips[tiles, low : low + count, :] = jnp.broadcast_to(energy, (count, LANES))
        low += count
    low = 0
    while low < used:
        count = min(LANES, used - low)
        block = turned[low : low + count, :]
        gram[:count, :columns] = lax.dot_general(
            block, record[...], (((1,), (1,)), ((), ())), preferred_element_type=jnp.float32
        )
        gram[:count, columns:] = lax.dot_general(
            block, rim[...], (((1,), (1,)), ((), ())), preferred_element_type=jnp.float32
        )
        for row in range(0, count, 8):
            line = pltpu.roll(gram[row : row + 8, :], (low + row) % width, 1, stride=1, stride_axis=0)
            for tile in range(tiles):
                strips[tile, low + row : low + row + 8, :] = line[:, tile * LANES : (tile + 1) * LANES]
        low += count

    def add_lags(tile, carry):
        value = strips[tile]
        stride = 1
        while stride < DELAYS:
            value = value[stride:] + value[:-stride]
            stride *= 2
        strips[tile, DELAYS:used, :] = value[1:]
        return carry

    lax.fori_loop(0, tiles + 1, add_lags, 0)
    factor = scale[0]
    for row in range(DELAYS, used, 16):
        halves = []
        for part in range(2):
            at = row + 8 * part
            line = jnp.concatenate([strips[tile, at : at + 8, :] for tile in range(tiles)], axis=1)
            line = pltpu.roll(line, (DELAYS - 1 - at) % width, 1)
            own = jnp.concatenate([strips[tiles, at : at + 8, :]] * tiles, axis=1)
            value = jnp.exp2(((own + norms[...]) - line) * factor)
            total = value[:, :LANES]
            for tile in range(1, tiles):
                total = total + value[:, tile * LANES : (tile + 1) * LANES]
            sums[at - DELAYS : at - DELAYS + 8, :] = total
            halves.append(value)
        weights[row - DELAYS : row - DELAYS + 16, :] = jnp.concatenate(halves, axis=0).astype(jnp.bfloat16)
    product = jnp.dot(weights[...], vectors[...], preferred_element_type=jnp.float32)
    lane = lax.broadcasted_iota(jnp.int32, (kept, 2 * LANES), 1)
    sub = lax.broadcasted_iota(jnp.int32, (kept, 2 * LANES), 0)
    product = jnp.where(lane // modes == sub % 8, product, 0.0)
    product = product[:, :LANES] + product[:, LANES:]
    product = product + pltpu.roll(product, 64, 1)
    product = product + pltpu.roll(product, 32, 1)
    lane = lax.broadcasted_iota(jnp.int32, (kept, LANES), 1)
    total = jnp.sum(sums[...], axis=1, keepdims=True)
    product = jnp.where(lane == modes, total, product)
    result[...] = jnp.where(lane <= modes, product, 0.0)
    share = PANEL // homes
    third = share // 3
    offset = meta[parts]
    for home in range(homes):
        start = kept - share * (home + 1) - offset
        packed = result[pl.ds(start, third), :]
        for part in range(1, 3):
            packed = packed + pltpu.roll(result[pl.ds(start + part * third, third), :], 40 * part, 1)
        out[home] = packed


def panel_call(homes, deal, shards, record, rim, vectors, norms, meta, scale):
    parts = len(shards)
    columns = record.shape[0]
    width = columns + LANES
    tiles = width // LANES
    used = -(-(PANEL + DELAYS - 1 + GROUP - 1) // GROUP) * GROUP
    kept = used - DELAYS
    share = PANEL // homes
    vm = pl.BlockSpec(memory_space=pltpu.VMEM)
    sm = pl.BlockSpec(memory_space=pltpu.SMEM)
    return pl.pallas_call(
        lambda *refs: panel_kernel(homes, parts, *refs),
        out_shape=jax.ShapeDtypeStruct((homes, share // 3, LANES), jnp.float32),
        in_specs=[sm, sm] + [vm] * (4 + parts),
        out_specs=vm,
        scratch_shapes=[
            pltpu.VMEM((homes * deal * GROUP, record.shape[1]), jnp.bfloat16),
            pltpu.VMEM((used, record.shape[1]), jnp.bfloat16),
            pltpu.VMEM((LANES, width), jnp.float32),
            pltpu.VMEM((tiles + 1, used, LANES), jnp.float32),
            pltpu.VMEM((kept, width), jnp.bfloat16),
            pltpu.VMEM((kept, LANES), jnp.float32),
            pltpu.VMEM((kept, LANES), jnp.float32),
        ],
        compiler_params=pltpu.CompilerParams(vmem_limit_bytes=56 * 1024 * 1024),
        cost_estimate=pl.CostEstimate(flops=2 * used * width * record.shape[1], bytes_accessed=8_000_000, transcendentals=kept * width),
    )(meta, scale, record, rim, vectors, norms, *shards)


def fan(vectors, width):
    columns, modes = vectors.shape
    padded = jnp.concatenate([vectors, jnp.zeros((width - columns, modes), vectors.dtype)], axis=0)
    return jnp.concatenate([jnp.roll(padded, shift, axis=0) for shift in range(8)], axis=1)


def slant(norms, width):
    padded = jnp.concatenate([norms, jnp.full((width - norms.shape[0],), BIG, jnp.float32)])
    return jnp.stack([jnp.roll(padded, shift) for shift in range(8)])


def pick_kernel(count, index, store, *outs):
    place = 0
    for out in outs:
        for row in range(out.shape[0]):
            at = index[place + row]

            @pl.when(at >= 0)
            def _():
                out[row] = store[at]

            @pl.when(at < 0)
            def _():
                out[row] = jnp.zeros(out.shape[1:], out.dtype)

        place += out.shape[0]


def pick(store, index, counts):
    vm = pl.BlockSpec(memory_space=pltpu.VMEM)
    sm = pl.BlockSpec(memory_space=pltpu.SMEM)
    return pl.pallas_call(
        lambda *refs: pick_kernel(counts, *refs),
        out_shape=[jax.ShapeDtypeStruct((count,) + store.shape[1:], store.dtype) for count in counts],
        in_specs=[sm, vm],
        out_specs=[vm] * len(counts),
    )(index, store)


def lag_sums(summed):
    stride = 1
    while stride < DELAYS:
        summed = summed[:-stride] + summed[stride:]
        stride = stride * 2
    return summed


def tour(homes):
    if homes == 8:
        return [0, 2, 4, 6, 7, 5, 3, 1]
    return list(range(homes))


def share_round(value):
    sharers = lax.axis_size("panel")
    found = [value]
    for hop in range(1, sharers):
        found.append(lax.ppermute(value, "panel", [((i + hop) % sharers, i) for i in range(sharers)]))
    rows = value.shape[0]
    first = (sharers - lax.axis_index("panel")) % sharers * rows
    return lax.dynamic_slice_in_dim(jnp.concatenate(found + found[:-1], axis=0), first, rows * sharers, 0)


def step_round(value, order, way):
    homes = len(order)
    return lax.ppermute(value, "tm", [(order[i], order[(i + way) % homes]) for i in range(homes)])


def body(record, eigvecs, starts, kernel_width):
    homes = lax.axis_size("tm")
    sharers = lax.axis_size("panel")
    home = lax.axis_index("tm")
    sharer = lax.axis_index("panel")
    columns, channels = record.shape
    width = columns + LANES
    groups = columns // GROUP
    turns = groups // (homes * sharers)
    deal = -(-(-(-(PANEL + DELAYS - 1 + GROUP - 1) // GROUP)) // homes)
    each = -(-deal // sharers)
    with jax.named_scope("deal_record"):
        cards = record.reshape(turns, sharers, homes, GROUP, channels)
        cards = lax.dynamic_index_in_dim(cards, sharer, 1, keepdims=False).transpose(1, 0, 2, 3)
        store = lax.all_to_all(cards, "tm", 0, 0).reshape(homes * turns, GROUP, channels)
    rim = lax.ppermute(record[columns - LANES :], "tm", [(i, i + 1) for i in range(homes - 1)])
    vectors = share_round(eigvecs)
    begins = share_round(starts) - (DELAYS - 1)
    with jax.named_scope("column_norms"):
        energy = jnp.sum(jnp.square(record.astype(jnp.float32)), axis=1)
        edge = jnp.sum(jnp.square(rim[LANES - DELAYS + 1 :].astype(jnp.float32)), axis=1)
        norms = slant(lag_sums(jnp.concatenate([edge, energy])), width)
        fanned = fan(vectors, width)
    with jax.named_scope("hand_over"):
        first = begins // GROUP
        opening = -((home - first) // homes)
        lowest = -((sharer - opening) // sharers)
        index = lowest[:, None] + jnp.arange(each)[None, :]
        index = jnp.where((index >= 0) & (index < homes * turns), index, -1).reshape(-1)
        sent = pick(store, index.astype(jnp.int32), [sharers * SLOTS * each])[0]
        sent = sent.reshape(sharers, SLOTS * each, GROUP, channels)
        held = lax.all_to_all(sent, "panel", 0, 0).reshape(sharers * SLOTS * each, GROUP, channels)
        own_first = starts - (DELAYS - 1)
        offset = own_first % GROUP
        own_first = own_first // GROUP
        own_opening = -((home - own_first) // homes)
        step = jnp.arange(deal)[None, :]
        index = ((own_opening[:, None] + step) % sharers) * (SLOTS * each) + jnp.arange(SLOTS)[:, None] * each
        index = index + step // sharers
        shards = pick(held, index.reshape(-1).astype(jnp.int32), [deal] * SLOTS)
    order = tour(homes)
    place_of = [order.index(i) for i in range(homes)]
    place = jnp.array(place_of, jnp.int32)[home]
    ring = jnp.array(order, jnp.int32)
    scale = -1.4426950408889634 / (kernel_width * (DELAYS * channels))
    results = []
    for slot in range(SLOTS):
        own = shards[slot]
        arrived = [(0, 0, own)]
        ahead = back = own
        for hop in range(1, homes // 2):
            ahead = step_round(ahead, order, 1)
            back = step_round(back, order, -1)
            arrived += [(-hop, 0, ahead), (hop, 0, back)]
        cut = (deal + 1) // 2
        arrived.append((homes // 2, 0, step_round(ahead[:cut], order, 1)))
        arrived.append((homes // 2, cut, step_round(back[cut:], order, -1)))
        meta = []
        for hop, skipped, _ in arrived:
            source = ring[(place + hop) % homes]
            meta.append((source - own_first[slot]) % homes + homes * skipped)
        meta.append(offset[slot])
        meta = jnp.stack(meta).astype(jnp.int32)
        parts = [part for _, _, part in arrived]
        with jax.named_scope("panel"):
            partial = panel_call(homes, deal, parts, record, rim, fanned, norms, meta, scale)
        results.append(lax.all_to_all(partial, "tm", 0, 0))
    finished = []
    for result in results:
        total = jnp.sum(result, axis=0)
        rows = jnp.concatenate([total[:, 40 * part : 40 * part + MODES + 1] for part in range(3)], axis=0)
        rows = jnp.flip(rows, axis=0)
        finished.append(rows[:, :MODES] / rows[:, MODES:])
    return jnp.stack(finished)


def solution(mesh):
    placed = (P("tm", None), P(("tm", "panel"), None), P("panel"), P())
    return jax.shard_map(
        body, mesh=mesh, in_specs=placed, out_specs=P("panel", "tm", None), check_vma=False
    )
```

```python
import jax
import jax.numpy as jnp
from jax import lax
from jax.experimental import pallas as pl
from jax.experimental.pallas import tpu as pltpu
from jax.sharding import PartitionSpec as P

DELAYS = 64
PANEL = 768
SLOTS = 2
GROUP = 16
LANES = 128
MODES = 32
BIG = 1e30


def panel_kernel(homes, slot, places, starts, scale, record, rim, vectors, norms, *rest):
    parts = len(places)
    shards = rest[:parts]
    out, window, turned, gram, strips, weights, sums, result = rest[parts:]
    columns = record.shape[0]
    width = columns + LANES
    tiles = width // LANES
    rows = window.shape[0]
    used = turned.shape[0]
    kept = used - DELAYS
    modes = MODES
    position = ring_position(homes)
    for number, (hop, skipped, deal) in enumerate(places):
        chunk = lax.rem(position + (hop % homes), homes)
        for step in range(shards[number].shape[0]):
            place = pl.multiple_of((chunk * deal + (skipped + step)) * GROUP, GROUP)
            window[pl.ds(place, GROUP), :] = shards[number][step]
    low = 0
    while low < used:
        count = min(LANES, used - low)
        turn = lax.broadcasted_iota(jnp.int32, (count, count), 0) + lax.broadcasted_iota(jnp.int32, (count, count), 1)
        flip = jnp.where(turn == count - 1, 2.0, 0.0).astype(jnp.bfloat16)
        block = jnp.dot(flip, window[used - low - count : used - low, :], preferred_element_type=jnp.float32)
        turned[low : low + count, :] = block.astype(jnp.bfloat16)
        energy = jnp.sum(block * block, axis=1, keepdims=True) * 0.25
        strips[tiles, low : low + count, :] = jnp.broadcast_to(energy, (count, LANES))
        low += count
    low = 0
    while low < used:
        count = min(LANES, used - low)
        block = turned[low : low + count, :]
        gram[:count, :columns] = lax.dot_general(
            block, record[...], (((1,), (1,)), ((), ())), preferred_element_type=jnp.float32
        )
        gram[:count, columns:] = lax.dot_general(
            block, rim[...], (((1,), (1,)), ((), ())), preferred_element_type=jnp.float32
        )
        for row in range(0, count, 8):
            line = pltpu.roll(gram[row : row + 8, :], (low + row) % width, 1, stride=1, stride_axis=0)
            for tile in range(tiles):
                strips[tile, low + row : low + row + 8, :] = line[:, tile * LANES : (tile + 1) * LANES]
        low += count

    def add_lags(tile, carry):
        value = strips[tile]
        stride = 1
        while stride < DELAYS:
            value = value[stride:] + value[:-stride]
            stride *= 2
        strips[tile, DELAYS:used, :] = value[1:]
        return carry

    lax.fori_loop(0, tiles + 1, add_lags, 0)
    factor = scale[0]
    for row in range(DELAYS, used, 16):
        halves = []
        for part in range(2):
            at = row + 8 * part
            line = jnp.concatenate([strips[tile, at : at + 8, :] for tile in range(tiles)], axis=1)
            line = pltpu.roll(line, (DELAYS - 1 - at) % width, 1)
            own = jnp.concatenate([strips[tiles, at : at + 8, :]] * tiles, axis=1)
            value = jnp.exp2(((own + norms[...]) - line) * factor)
            total = value[:, :LANES]
            for tile in range(1, tiles):
                total = total + value[:, tile * LANES : (tile + 1) * LANES]
            sums[at - DELAYS : at - DELAYS + 8, :] = total
            halves.append(value)
        weights[row - DELAYS : row - DELAYS + 16, :] = jnp.concatenate(halves, axis=0).astype(jnp.bfloat16)
    product = jnp.dot(weights[...], vectors[...], preferred_element_type=jnp.float32)
    lane = lax.broadcasted_iota(jnp.int32, (kept, 2 * LANES), 1)
    sub = lax.broadcasted_iota(jnp.int32, (kept, 2 * LANES), 0)
    product = jnp.where(lane // modes == sub % 8, product, 0.0)
    product = product[:, :LANES] + product[:, LANES:]
    product = product + pltpu.roll(product, 64, 1)
    product = product + pltpu.roll(product, 32, 1)
    lane = lax.broadcasted_iota(jnp.int32, (kept, LANES), 1)
    total = jnp.sum(sums[...], axis=1, keepdims=True)
    product = jnp.where(lane == modes, total, product)
    result[...] = jnp.where(lane <= modes, product, 0.0)
    share = PANEL // homes
    third = share // 3
    offset = lax.bitwise_and(starts[slot] - (DELAYS - 1), GROUP - 1)
    for home in range(homes):
        start = kept - share * (home + 1) - offset
        packed = result[pl.ds(start, third), :]
        for part in range(1, 3):
            packed = packed + pltpu.roll(result[pl.ds(start + part * third, third), :], 40 * part, 1)
        out[home] = packed


def panel_call(homes, slot, arrived, record, rim, vectors, norms, starts, scale):
    deal = arrived[0][2].shape[0]
    parts = len(arrived)
    places = [(hop, skipped, deal) for hop, skipped, _ in arrived]
    shards = [part for _, _, part in arrived]
    columns = record.shape[0]
    width = columns + LANES
    tiles = width // LANES
    used = -(-(PANEL + DELAYS - 1 + GROUP - 1) // GROUP) * GROUP
    kept = used - DELAYS
    share = PANEL // homes
    vm = pl.BlockSpec(memory_space=pltpu.VMEM)
    sm = pl.BlockSpec(memory_space=pltpu.SMEM)
    return pl.pallas_call(
        lambda *refs: panel_kernel(homes, slot, places, *refs),
        out_shape=jax.ShapeDtypeStruct((homes, share // 3, LANES), jnp.float32),
        in_specs=[sm, sm] + [vm] * (4 + parts),
        out_specs=vm,
        scratch_shapes=[
            pltpu.VMEM((homes * deal * GROUP, record.shape[1]), jnp.bfloat16),
            pltpu.VMEM((used, record.shape[1]), jnp.bfloat16),
            pltpu.VMEM((LANES, width), jnp.float32),
            pltpu.VMEM((tiles + 1, used, LANES), jnp.float32),
            pltpu.VMEM((kept, width), jnp.bfloat16),
            pltpu.VMEM((kept, LANES), jnp.float32),
            pltpu.VMEM((kept, LANES), jnp.float32),
        ],
        compiler_params=pltpu.CompilerParams(vmem_limit_bytes=56 * 1024 * 1024),
        cost_estimate=pl.CostEstimate(flops=2 * used * width * record.shape[1], bytes_accessed=8_000_000, transcendentals=kept * width),
    )(starts, scale, record, rim, vectors, norms, *shards)


def ring_position(homes):
    home = lax.axis_index("tm")
    if homes != 8:
        return home
    return jnp.where(lax.bitwise_and(home, 1) == 0, home, 2 * homes - 1 - home) // 2


def tour(homes):
    if homes != 8:
        return list(range(homes))
    return [0, 2, 4, 6, 7, 5, 3, 1]


def step_round(value, way):
    homes = lax.axis_size("tm")
    order = tour(homes)
    return lax.ppermute(value, "tm", [(order[i], order[(i + way) % homes]) for i in range(homes)])


def own_kernel(homes, deal, starts, record, *outs):
    home = lax.axis_index("tm")
    position = ring_position(homes)
    held = record.shape[0] // GROUP
    for slot in range(SLOTS):
        first = lax.shift_right_arithmetic(starts[slot] - (DELAYS - 1), 4) - home * held
        for hop in range(homes):
            out = outs[slot * homes + hop]
            chunk = lax.rem(position + hop, homes)
            for step in range(deal):
                group = first + chunk * deal + step
                inside = (group >= 0) & (group < held)

                @pl.when(inside)
                def _():
                    out[step] = record[pl.ds(pl.multiple_of(group * GROUP, GROUP), GROUP), :]

                @pl.when(jnp.logical_not(inside))
                def _():
                    out[step] = jnp.zeros(out.shape[1:], out.dtype)


def own_rows(homes, deal, starts, record):
    vm = pl.BlockSpec(memory_space=pltpu.VMEM)
    sm = pl.BlockSpec(memory_space=pltpu.SMEM)
    shape = jax.ShapeDtypeStruct((deal, GROUP, record.shape[1]), record.dtype)
    flat = pl.pallas_call(
        lambda *refs: own_kernel(homes, deal, *refs),
        out_shape=[shape] * (SLOTS * homes),
        in_specs=[sm, vm],
        out_specs=[vm] * (SLOTS * homes),
        compiler_params=pltpu.CompilerParams(vmem_limit_bytes=40 * 1024 * 1024),
    )(starts, record)
    return [flat[slot * homes : (slot + 1) * homes] for slot in range(SLOTS)]


def prepare_kernel(record, rim, *rest):
    pieces = rest[:-4]
    norms, fanned, energy, spread = rest[-4:]
    columns = record.shape[0]
    width = columns + LANES
    sharers = len(pieces)
    sharer = lax.axis_index("panel")
    for source, low, high in ((record, 0, columns), (rim, columns, width)):
        for row in range(low, high, LANES):
            value = source[row - low : row - low + LANES, :].astype(jnp.float32)
            value = value * value
            total = value[:, :LANES]
            for lane in range(LANES, value.shape[1], LANES):
                total = total + value[:, lane : lane + LANES]
            energy[:, row : row + LANES] = lax.dot_general(
                jnp.ones((8, LANES), jnp.float32),
                total,
                (((1,), (1,)), ((), ())),
                precision=lax.Precision.HIGHEST,
                preferred_element_type=jnp.float32,
            )
    value = energy[...]
    stride = 1
    while stride < DELAYS:
        value = value + pltpu.roll(value, stride, 1)
        stride *= 2
    lane = lax.broadcasted_iota(jnp.int32, (8, width), 1)
    value = jnp.where(lane < columns, value, BIG)
    norms[...] = pltpu.roll(value, 0, 1, stride=1, stride_axis=0)
    lane = lax.broadcasted_iota(jnp.int32, (MODES, LANES), 1)
    mode = lax.broadcasted_iota(jnp.int32, (MODES, LANES), 0)
    copies = jnp.where(lax.bitwise_and(lane, MODES - 1) == mode, 1.0, 0.0).astype(jnp.bfloat16)
    rows = columns // sharers
    for hop in range(sharers):
        place = pl.multiple_of(lax.rem(sharer + hop, sharers) * rows, rows)
        spread[pl.ds(place, rows), :] = jnp.dot(pieces[hop][...], copies, preferred_element_type=jnp.float32)
    spread[columns:, :] = jnp.zeros((LANES, LANES), jnp.float32)
    value = spread[...]
    block = lax.broadcasted_iota(jnp.int32, (width, LANES), 1) // MODES
    per = LANES // MODES
    for half in range(2):
        result = jnp.zeros((width, LANES), jnp.float32)
        for part in range(per):
            result = jnp.where(block == part, pltpu.roll(value, half * per + part, 0), result)
        fanned[:, half * LANES : (half + 1) * LANES] = result.astype(jnp.bfloat16)


def prepare(record, rim, pieces):
    width = record.shape[0] + LANES
    vm = pl.BlockSpec(memory_space=pltpu.VMEM)
    return pl.pallas_call(
        prepare_kernel,
        out_shape=[
            jax.ShapeDtypeStruct((8, width), jnp.float32),
            jax.ShapeDtypeStruct((width, 2 * LANES), jnp.bfloat16),
        ],
        in_specs=[vm] * (2 + len(pieces)),
        out_specs=[vm] * 2,
        scratch_shapes=[pltpu.VMEM((8, width), jnp.float32), pltpu.VMEM((width, LANES), jnp.float32)],
        compiler_params=pltpu.CompilerParams(vmem_limit_bytes=40 * 1024 * 1024),
    )(record, rim, *pieces)


def body(record, eigvecs, starts, kernel_width):
    homes = lax.axis_size("tm")
    sharers = lax.axis_size("panel")
    columns, channels = record.shape
    groups = -(-(PANEL + DELAYS - 1 + GROUP - 1) // GROUP)
    deal = -(-groups // homes)
    half = homes // 2
    cut = (deal + 1) // 2
    with jax.named_scope("own_rows"):
        chunks = own_rows(homes, deal, starts, record)
    shards = []
    for slot in range(SLOTS):
        with jax.named_scope("scatter"):
            mine = chunks[slot]
            ahead = step_round(mine[half][:cut], 1)
            back = step_round(mine[half][cut:], -1)
            ahead = mine[half - 1].at[:cut].add(ahead)
            back = mine[half + 1].at[cut:].add(back)
            for hop in range(half - 2, -1, -1):
                ahead = mine[hop] + step_round(ahead, 1)
                back = step_round(back, -1)
                back = back if hop == 0 else mine[homes - hop] + back
            shards.append(ahead + back)
    rim = lax.ppermute(record[columns - LANES :], "tm", [(i, i + 1) for i in range(homes - 1)])
    pieces = [eigvecs]
    for hop in range(1, sharers):
        pieces.append(lax.ppermute(eigvecs, "panel", [((i + hop) % sharers, i) for i in range(sharers)]))
    with jax.named_scope("prepare"):
        norms, fanned = prepare(record, rim, pieces)
    scale = -1.4426950408889634 / (kernel_width * (DELAYS * channels))
    results = []
    for slot in range(SLOTS):
        with jax.named_scope("gather"):
            ahead = back = shards[slot]
            arrived = [(0, 0, ahead)]
            for hop in range(1, half):
                ahead = step_round(ahead, 1)
                back = step_round(back, -1)
                arrived += [(-hop, 0, ahead), (hop, 0, back)]
            arrived.append((half, 0, step_round(ahead[:cut], 1)))
            arrived.append((half, cut, step_round(back[cut:], -1)))
        with jax.named_scope("panel"):
            partial = panel_call(homes, slot, arrived, record, rim, fanned, norms, starts, scale)
        results.append(lax.all_to_all(partial, "tm", 0, 0))
    finished = []
    for result in results:
        total = jnp.sum(result, axis=0)
        rows = jnp.concatenate([total[:, 40 * part : 40 * part + MODES + 1] for part in range(3)], axis=0)
        rows = jnp.flip(rows, axis=0)
        finished.append(rows[:, :MODES] / rows[:, MODES:])
    return jnp.stack(finished)


def solution(mesh):
    placed = (P("tm", None), P(("tm", "panel"), None), P("panel"), P())
    return jax.shard_map(
        body, mesh=mesh, in_specs=placed, out_specs=P("panel", "tm", None), check_vma=False
    )
```

```python
import jax
import jax.numpy as jnp
from jax import lax
from jax.experimental import pallas as pl
from jax.experimental.pallas import tpu as pltpu
from jax.sharding import PartitionSpec as P

DELAYS = 64
PANEL = 768
SLOTS = 2
GROUP = 16
LANES = 128
MODES = 32
BIG = 1e30


def panel_kernel(homes, places, starts, scale, record, rim, vectors, norms, *rest):
    parts = len(places)
    shards = [rest[slot * parts : (slot + 1) * parts] for slot in range(SLOTS)]
    out, window, turned, energies, gram, strips, weights, sums, result = rest[SLOTS * parts :]
    columns = record.shape[0]
    width = columns + LANES
    tiles = width // LANES
    used = turned.shape[1]
    kept = used - DELAYS
    position = ring_position(homes)
    share = PANEL // homes
    third = share // 3
    factor = scale[0]

    def collect(slot):
        for number, (hop, skipped, deal) in enumerate(places):
            chunk = lax.rem(position + (hop % homes), homes)
            shard = shards[slot][number]
            for step in range(0, shard.shape[0], GROUP):
                place = pl.multiple_of(chunk * deal + (skipped + step), GROUP)
                window[pl.ds(place, GROUP), :] = shard[step : step + GROUP, :]
        low = 0
        while low < used:
            count = min(LANES, used - low)
            turn = lax.broadcasted_iota(jnp.int32, (count, count), 0) + lax.broadcasted_iota(jnp.int32, (count, count), 1)
            flip = jnp.where(turn == count - 1, 2.0, 0.0).astype(jnp.bfloat16)
            block = jnp.dot(flip, window[used - low - count : used - low, :], preferred_element_type=jnp.float32)
            turned[slot, low : low + count, :] = block.astype(jnp.bfloat16)
            energy = jnp.sum(block * block, axis=1, keepdims=True) * 0.25
            energies[slot, low : low + count, :] = jnp.broadcast_to(energy, (count, LANES))
            low += count

    def product_with(slot, rows):
        return lax.dot_general(
            turned[slot], rows, (((1,), (1,)), ((), ())), preferred_element_type=jnp.float32
        )

    def turn_rows():
        for row in range(0, used, 8):
            line = pltpu.roll(gram[row : row + 8, :], row % width, 1, stride=1, stride_axis=0)
            for tile in range(tiles):
                strips[tile, row : row + 8, :] = line[:, tile * LANES : (tile + 1) * LANES]

    def add_lags(tile):
        value = strips[tile, 1:, :] + strips[tile, : used - 1, :]
        stride = 2
        while stride < DELAYS:
            value = value[stride:] + value[:-stride]
            stride *= 2
        strips[tile, DELAYS:used, :] = value[1:]

    def weigh(slot):
        for row in range(DELAYS, used, 16):
            halves = []
            for part in range(2):
                at = row + 8 * part
                line = jnp.concatenate([strips[tile, at : at + 8, :] for tile in range(tiles)], axis=1)
                line = pltpu.roll(line, (DELAYS - 1 - at) % width, 1)
                own = jnp.concatenate([strips[tiles, at : at + 8, :]] * tiles, axis=1)
                value = jnp.exp2(((own + norms[...]) - line) * factor)
                total = value[:, :LANES]
                for tile in range(1, tiles):
                    total = total + value[:, tile * LANES : (tile + 1) * LANES]
                sums[at - DELAYS : at - DELAYS + 8, :] = total
                halves.append(value)
            weights[row - DELAYS : row - DELAYS + 16, :] = jnp.concatenate(halves, axis=0).astype(jnp.bfloat16)
        product = jnp.dot(weights[...], vectors[...], preferred_element_type=jnp.float32)
        lane = lax.broadcasted_iota(jnp.int32, (kept, 2 * LANES), 1)
        sub = lax.broadcasted_iota(jnp.int32, (kept, 2 * LANES), 0)
        product = jnp.where(lane // MODES == sub % 8, product, 0.0)
        product = product[:, :LANES] + product[:, LANES:]
        product = product + pltpu.roll(product, 64, 1)
        product = product + pltpu.roll(product, 32, 1)
        lane = lax.broadcasted_iota(jnp.int32, (kept, LANES), 1)
        total = jnp.sum(sums[...], axis=1, keepdims=True)
        product = jnp.where(lane == MODES, total, product)
        result[...] = jnp.where(lane <= MODES, product, 0.0)
        offset = lax.bitwise_and(starts[slot] - (DELAYS - 1), GROUP - 1)
        for home in range(homes):
            start = kept - share * (home + 1) - offset
            packed = result[pl.ds(start, third), :]
            for part in range(1, 3):
                packed = packed + pltpu.roll(result[pl.ds(start + part * third, third), :], 40 * part, 1)
            out[home, slot * third : (slot + 1) * third, :] = packed

    for slot in range(SLOTS):
        collect(slot)
    gram[:, :columns] = product_with(0, record[...])
    gram[:, columns:] = product_with(0, rim[...])
    for slot in range(SLOTS):
        turn_rows()
        strips[tiles] = energies[slot]
        if slot + 1 < SLOTS:

            def add_and_multiply(pair, carry):
                add_lags(2 * pair)
                add_lags(2 * pair + 1)
                part = pl.ds(pl.multiple_of(pair * 2 * LANES, 2 * LANES), 2 * LANES)
                gram[:, part] = product_with(slot + 1, record[part, :])
                return carry

            lax.fori_loop(0, tiles // 2, add_and_multiply, 0)
            gram[:, columns:] = product_with(slot + 1, rim[...])
            add_lags(tiles - 1)
            add_lags(tiles)
        else:

            def add_only(tile, carry):
                add_lags(tile)
                return carry

            lax.fori_loop(0, tiles + 1, add_only, 0)
        weigh(slot)


def panel_call(homes, arrived, record, rim, vectors, norms, starts, scale):
    deal = arrived[0][0][2].shape[0]
    parts = len(arrived[0])
    places = [(hop, skipped, deal) for hop, skipped, _ in arrived[0]]
    shards = [part for slot in range(SLOTS) for _, _, part in arrived[slot]]
    columns = record.shape[0]
    width = columns + LANES
    tiles = width // LANES
    used = -(-(PANEL + DELAYS - 1 + GROUP - 1) // GROUP) * GROUP
    kept = used - DELAYS
    share = PANEL // homes
    vm = pl.BlockSpec(memory_space=pltpu.VMEM)
    sm = pl.BlockSpec(memory_space=pltpu.SMEM)
    return pl.pallas_call(
        lambda *refs: panel_kernel(homes, places, *refs),
        out_shape=jax.ShapeDtypeStruct((homes, SLOTS * (share // 3), LANES), jnp.float32),
        in_specs=[sm, sm] + [vm] * (4 + SLOTS * parts),
        out_specs=vm,
        scratch_shapes=[
            pltpu.VMEM((homes * deal, record.shape[1]), jnp.bfloat16),
            pltpu.VMEM((SLOTS, used, record.shape[1]), jnp.bfloat16),
            pltpu.VMEM((SLOTS, used, LANES), jnp.float32),
            pltpu.VMEM((used, width), jnp.float32),
            pltpu.VMEM((tiles + 1, used, LANES), jnp.float32),
            pltpu.VMEM((kept, width), jnp.bfloat16),
            pltpu.VMEM((kept, LANES), jnp.float32),
            pltpu.VMEM((kept, LANES), jnp.float32),
        ],
        compiler_params=pltpu.CompilerParams(vmem_limit_bytes=56 * 1024 * 1024),
        cost_estimate=pl.CostEstimate(
            flops=2 * SLOTS * used * width * record.shape[1], bytes_accessed=10_000_000, transcendentals=SLOTS * kept * width
        ),
    )(starts, scale, record, rim, vectors, norms, *shards)


def ring_position(homes):
    home = lax.axis_index("tm")
    if homes != 8:
        return home
    return jnp.where(lax.bitwise_and(home, 1) == 0, home, 2 * homes - 1 - home) // 2


def tour(homes):
    if homes != 8:
        return list(range(homes))
    return [0, 2, 4, 6, 7, 5, 3, 1]


def step_round(value, way):
    homes = lax.axis_size("tm")
    order = tour(homes)
    return lax.ppermute(value, "tm", [(order[i], order[(i + way) % homes]) for i in range(homes)])


def own_kernel(homes, deal, starts, record, *outs):
    home = lax.axis_index("tm")
    position = ring_position(homes)
    held = record.shape[0] // GROUP
    for slot in range(SLOTS):
        first = lax.shift_right_arithmetic(starts[slot] - (DELAYS - 1), 4) - home * held
        for hop in range(homes):
            out = outs[slot * homes + hop]
            chunk = lax.rem(position + hop, homes)
            for step in range(deal):
                group = first + chunk * deal + step
                inside = (group >= 0) & (group < held)

                place = slice(step * GROUP, (step + 1) * GROUP)

                @pl.when(inside)
                def _():
                    out[place, :] = record[pl.ds(pl.multiple_of(group * GROUP, GROUP), GROUP), :]

                @pl.when(jnp.logical_not(inside))
                def _():
                    out[place, :] = jnp.zeros((GROUP, out.shape[1]), out.dtype)


def own_rows(homes, deal, starts, record):
    vm = pl.BlockSpec(memory_space=pltpu.VMEM)
    sm = pl.BlockSpec(memory_space=pltpu.SMEM)
    shape = jax.ShapeDtypeStruct((deal * GROUP, record.shape[1]), record.dtype)
    flat = pl.pallas_call(
        lambda *refs: own_kernel(homes, deal, *refs),
        out_shape=[shape] * (SLOTS * homes),
        in_specs=[sm, vm],
        out_specs=[vm] * (SLOTS * homes),
        compiler_params=pltpu.CompilerParams(vmem_limit_bytes=40 * 1024 * 1024),
    )(starts, record)
    return [flat[slot * homes : (slot + 1) * homes] for slot in range(SLOTS)]


def prepare_kernel(record, rim, *rest):
    pieces = rest[:-4]
    norms, fanned, energy, spread = rest[-4:]
    columns = record.shape[0]
    width = columns + LANES
    sharers = len(pieces)
    sharer = lax.axis_index("panel")
    for source, low, high in ((record, 0, columns), (rim, columns, width)):
        for row in range(low, high, LANES):
            value = source[row - low : row - low + LANES, :].astype(jnp.float32)
            value = value * value
            total = value[:, :LANES]
            for lane in range(LANES, value.shape[1], LANES):
                total = total + value[:, lane : lane + LANES]
            energy[:, row : row + LANES] = lax.dot_general(
                jnp.ones((8, LANES), jnp.float32),
                total,
                (((1,), (1,)), ((), ())),
                precision=lax.Precision.HIGHEST,
                preferred_element_type=jnp.float32,
            )
    value = energy[...]
    stride = 1
    while stride < DELAYS:
        value = value + pltpu.roll(value, stride, 1)
        stride *= 2
    lane = lax.broadcasted_iota(jnp.int32, (8, width), 1)
    value = jnp.where(lane < columns, value, BIG)
    norms[...] = pltpu.roll(value, 0, 1, stride=1, stride_axis=0)
    lane = lax.broadcasted_iota(jnp.int32, (MODES, LANES), 1)
    mode = lax.broadcasted_iota(jnp.int32, (MODES, LANES), 0)
    copies = jnp.where(lax.bitwise_and(lane, MODES - 1) == mode, 1.0, 0.0).astype(jnp.bfloat16)
    rows = columns // sharers
    for hop in range(sharers):
        place = pl.multiple_of(lax.rem(sharer + hop, sharers) * rows, rows)
        spread[pl.ds(place, rows), :] = jnp.dot(pieces[hop][...], copies, preferred_element_type=jnp.float32)
    spread[columns:, :] = jnp.zeros((LANES, LANES), jnp.float32)
    value = spread[...]
    block = lax.broadcasted_iota(jnp.int32, (width, LANES), 1) // MODES
    per = LANES // MODES
    for half in range(2):
        result = jnp.zeros((width, LANES), jnp.float32)
        for part in range(per):
            result = jnp.where(block == part, pltpu.roll(value, half * per + part, 0), result)
        fanned[:, half * LANES : (half + 1) * LANES] = result.astype(jnp.bfloat16)


def prepare(record, rim, pieces):
    width = record.shape[0] + LANES
    vm = pl.BlockSpec(memory_space=pltpu.VMEM)
    return pl.pallas_call(
        prepare_kernel,
        out_shape=[
            jax.ShapeDtypeStruct((8, width), jnp.float32),
            jax.ShapeDtypeStruct((width, 2 * LANES), jnp.bfloat16),
        ],
        in_specs=[vm] * (2 + len(pieces)),
        out_specs=[vm] * 2,
        scratch_shapes=[pltpu.VMEM((8, width), jnp.float32), pltpu.VMEM((width, LANES), jnp.float32)],
        compiler_params=pltpu.CompilerParams(vmem_limit_bytes=40 * 1024 * 1024),
    )(record, rim, *pieces)


def body(record, eigvecs, starts, kernel_width):
    homes = lax.axis_size("tm")
    sharers = lax.axis_size("panel")
    columns, channels = record.shape
    groups = -(-(PANEL + DELAYS - 1 + GROUP - 1) // GROUP)
    deal = -(-groups // homes)
    half = homes // 2
    cut = (deal + 1) // 2 * GROUP
    with jax.named_scope("own_rows"):
        chunks = own_rows(homes, deal, starts, record)
    shards = []
    for slot in range(SLOTS):
        with jax.named_scope("scatter"):
            mine = chunks[slot]
            ahead = step_round(mine[half][:cut], 1)
            back = step_round(mine[half][cut:], -1)
            ahead = mine[half - 1].at[:cut].add(ahead)
            back = mine[half + 1].at[cut:].add(back)
            for hop in range(half - 2, -1, -1):
                ahead = mine[hop] + step_round(ahead, 1)
                back = step_round(back, -1)
                back = back if hop == 0 else mine[homes - hop] + back
            shards.append(ahead + back)
    rim = lax.ppermute(record[columns - LANES :], "tm", [(i, i + 1) for i in range(homes - 1)])
    pieces = [eigvecs]
    for hop in range(1, sharers):
        pieces.append(lax.ppermute(eigvecs, "panel", [((i + hop) % sharers, i) for i in range(sharers)]))
    with jax.named_scope("prepare"):
        norms, fanned = prepare(record, rim, pieces)
        shards, norms, fanned = lax.optimization_barrier((shards, norms, fanned))
    scale = -1.4426950408889634 / (kernel_width * (DELAYS * channels))
    results = []
    with jax.named_scope("gather"):
        for slot in range(SLOTS):
            ahead = back = shards[slot]
            arrived = [(0, 0, ahead)]
            for hop in range(1, half):
                ahead = step_round(ahead, 1)
                back = step_round(back, -1)
                arrived += [(-hop, 0, ahead), (hop, 0, back)]
            arrived.append((half, 0, step_round(ahead[:cut], 1)))
            arrived.append((half, cut, step_round(back[cut:], -1)))
            results.append(arrived)
    with jax.named_scope("panels"):
        partial = panel_call(homes, results, record, rim, fanned, norms, starts, scale)
    total = jnp.sum(lax.all_to_all(partial, "tm", 0, 0), axis=0)
    third = total.shape[0] // SLOTS
    finished = []
    for slot in range(SLOTS):
        own = total[slot * third : (slot + 1) * third]
        rows = jnp.concatenate([own[:, 40 * part : 40 * part + MODES + 1] for part in range(3)], axis=0)
        rows = jnp.flip(rows, axis=0)
        finished.append(rows[:, :MODES] / rows[:, MODES:])
    return jnp.stack(finished)


def solution(mesh):
    placed = (P("tm", None), P(("tm", "panel"), None), P("panel"), P())
    return jax.shard_map(
        body, mesh=mesh, in_specs=placed, out_specs=P("panel", "tm", None), check_vma=False
    )
```

```python
import jax
import jax.numpy as jnp
from jax import lax
from jax.experimental import pallas as pl
from jax.experimental.pallas import tpu as pltpu
from jax.sharding import PartitionSpec as P

DELAYS = 64
PANEL = 768
SLOTS = 2
GROUP = 16
LANES = 128
MODES = 32
BIG = 1e30


def panel_kernel(homes, places, starts, scale, record, rim, vectors, norms, *rest):
    parts = len(places)
    shards = [rest[slot * parts : (slot + 1) * parts] for slot in range(SLOTS)]
    out, window, turned, energies, gram, strips, weights, sums, result = rest[SLOTS * parts :]
    columns = record.shape[0]
    width = columns + LANES
    tiles = width // LANES
    used = turned.shape[1]
    kept = used - DELAYS
    position = ring_position(homes)
    share = PANEL // homes
    third = share // 3
    factor = scale[0]

    def collect(slot):
        for number, (hop, skipped, deal) in enumerate(places):
            chunk = lax.rem(position + (hop % homes), homes)
            shard = shards[slot][number]
            for step in range(0, shard.shape[0], GROUP):
                place = pl.multiple_of(chunk * deal + (skipped + step), GROUP)
                window[pl.ds(place, GROUP), :] = shard[step : step + GROUP, :]
        low = 0
        while low < used:
            count = min(LANES, used - low)
            turn = lax.broadcasted_iota(jnp.int32, (count, count), 0) + lax.broadcasted_iota(jnp.int32, (count, count), 1)
            flip = jnp.where(turn == count - 1, 2.0, 0.0).astype(jnp.bfloat16)
            block = jnp.dot(flip, window[used - low - count : used - low, :], preferred_element_type=jnp.float32)
            turned[slot, low : low + count, :] = block.astype(jnp.bfloat16)
            energy = jnp.sum(block * block, axis=1, keepdims=True) * 0.25
            energies[slot, low : low + count, :] = jnp.broadcast_to(energy, (count, LANES))
            low += count

    def product_with(slot, rows):
        return lax.dot_general(
            turned[slot], rows, (((1,), (1,)), ((), ())), preferred_element_type=jnp.float32
        )

    def turn_rows(slot):
        for row in range(0, used, 8):
            line = pltpu.roll(gram[slot, row : row + 8, :], row % width, 1, stride=1, stride_axis=0)
            for tile in range(tiles):
                strips[tile, row : row + 8, :] = line[:, tile * LANES : (tile + 1) * LANES]

    def add_lags(tile):
        value = strips[tile, :, :]
        stride = 32
        while stride >= 2:
            value = value[stride:] + value[:-stride]
            stride //= 2
        value = value[1:] + value[:-1]
        strips[tile, DELAYS:used, :] = value[1:]

    def weigh(slot):
        for row in range(DELAYS, used, 16):
            halves = []
            for part in range(2):
                at = row + 8 * part
                line = jnp.concatenate([strips[tile, at : at + 8, :] for tile in range(tiles)], axis=1)
                line = pltpu.roll(line, (DELAYS - 1 - at) % width, 1)
                own = jnp.concatenate([strips[tiles, at : at + 8, :]] * tiles, axis=1)
                value = jnp.exp2(((own + norms[...]) - line) * factor)
                total = value[:, :LANES]
                for tile in range(1, tiles):
                    total = total + value[:, tile * LANES : (tile + 1) * LANES]
                sums[at - DELAYS : at - DELAYS + 8, :] = total
                halves.append(value)
            weights[row - DELAYS : row - DELAYS + 16, :] = jnp.concatenate(halves, axis=0).astype(jnp.bfloat16)
        product = jnp.dot(weights[...], vectors[...], preferred_element_type=jnp.float32)
        lane = lax.broadcasted_iota(jnp.int32, (kept, 2 * LANES), 1)
        sub = lax.broadcasted_iota(jnp.int32, (kept, 2 * LANES), 0)
        product = jnp.where(lane // MODES == sub % 8, product, 0.0)
        product = product[:, :LANES] + product[:, LANES:]
        product = product + pltpu.roll(product, 64, 1)
        product = product + pltpu.roll(product, 32, 1)
        lane = lax.broadcasted_iota(jnp.int32, (kept, LANES), 1)
        total = jnp.sum(sums[...], axis=1, keepdims=True)
        product = jnp.where(lane == MODES, total, product)
        result[...] = jnp.where(lane <= MODES, product, 0.0)
        offset = lax.bitwise_and(starts[slot] - (DELAYS - 1), GROUP - 1)
        for home in range(homes):
            start = kept - share * (home + 1) - offset
            packed = result[pl.ds(start, third), :]
            for part in range(1, 3):
                packed = packed + pltpu.roll(result[pl.ds(start + part * third, third), :], 40 * part, 1)
            out[home, slot * third : (slot + 1) * third, :] = packed

    for slot in range(SLOTS):
        collect(slot)
    for slot in range(SLOTS):
        gram[slot, :, :columns] = product_with(slot, record[...])
        gram[slot, :, columns:] = product_with(slot, rim[...])
    for slot in range(SLOTS):
        turn_rows(slot)
        strips[tiles] = energies[slot]
        for tile in range(tiles + 1):
            add_lags(tile)
        weigh(slot)


def panel_call(homes, arrived, record, rim, vectors, norms, starts, scale):
    deal = arrived[0][0][2].shape[0]
    parts = len(arrived[0])
    places = [(hop, skipped, deal) for hop, skipped, _ in arrived[0]]
    shards = [part for slot in range(SLOTS) for _, _, part in arrived[slot]]
    columns = record.shape[0]
    width = columns + LANES
    tiles = width // LANES
    used = -(-(PANEL + DELAYS - 1 + GROUP - 1) // GROUP) * GROUP
    kept = used - DELAYS
    share = PANEL // homes
    vm = pl.BlockSpec(memory_space=pltpu.VMEM)
    sm = pl.BlockSpec(memory_space=pltpu.SMEM)
    return pl.pallas_call(
        lambda *refs: panel_kernel(homes, places, *refs),
        out_shape=jax.ShapeDtypeStruct((homes, SLOTS * (share // 3), LANES), jnp.float32),
        in_specs=[sm, sm] + [vm] * (4 + SLOTS * parts),
        out_specs=vm,
        scratch_shapes=[
            pltpu.VMEM((homes * deal, record.shape[1]), jnp.bfloat16),
            pltpu.VMEM((SLOTS, used, record.shape[1]), jnp.bfloat16),
            pltpu.VMEM((SLOTS, used, LANES), jnp.float32),
            pltpu.VMEM((SLOTS, used, width), jnp.float32),
            pltpu.VMEM((tiles + 1, used, LANES), jnp.float32),
            pltpu.VMEM((kept, width), jnp.bfloat16),
            pltpu.VMEM((kept, LANES), jnp.float32),
            pltpu.VMEM((kept, LANES), jnp.float32),
        ],
        compiler_params=pltpu.CompilerParams(vmem_limit_bytes=46 * 1024 * 1024),
        cost_estimate=pl.CostEstimate(
            flops=2 * SLOTS * used * width * record.shape[1], bytes_accessed=10_000_000, transcendentals=SLOTS * kept * width
        ),
    )(starts, scale, record, rim, vectors, norms, *shards)


def ring_position(homes):
    home = lax.axis_index("tm")
    if homes != 8:
        return home
    return jnp.where(lax.bitwise_and(home, 1) == 0, home, 2 * homes - 1 - home) // 2


def tour(homes):
    if homes != 8:
        return list(range(homes))
    return [0, 2, 4, 6, 7, 5, 3, 1]


def step_round(value, way):
    homes = lax.axis_size("tm")
    order = tour(homes)
    return lax.ppermute(value, "tm", [(order[i], order[(i + way) % homes]) for i in range(homes)])


def own_kernel(homes, deal, starts, record, *outs):
    home = lax.axis_index("tm")
    position = ring_position(homes)
    held = record.shape[0] // GROUP
    for slot in range(SLOTS):
        first = lax.shift_right_arithmetic(starts[slot] - (DELAYS - 1), 4) - home * held
        for hop in range(homes):
            out = outs[slot * homes + hop]
            chunk = lax.rem(position + hop, homes)
            for step in range(deal):
                group = first + chunk * deal + step
                inside = (group >= 0) & (group < held)

                place = slice(step * GROUP, (step + 1) * GROUP)

                @pl.when(inside)
                def _():
                    out[place, :] = record[pl.ds(pl.multiple_of(group * GROUP, GROUP), GROUP), :]

                @pl.when(jnp.logical_not(inside))
                def _():
                    out[place, :] = jnp.zeros((GROUP, out.shape[1]), out.dtype)


def own_rows(homes, deal, starts, record):
    vm = pl.BlockSpec(memory_space=pltpu.VMEM)
    sm = pl.BlockSpec(memory_space=pltpu.SMEM)
    shape = jax.ShapeDtypeStruct((deal * GROUP, record.shape[1]), record.dtype)
    flat = pl.pallas_call(
        lambda *refs: own_kernel(homes, deal, *refs),
        out_shape=[shape] * (SLOTS * homes),
        in_specs=[sm, vm],
        out_specs=[vm] * (SLOTS * homes),
        compiler_params=pltpu.CompilerParams(vmem_limit_bytes=40 * 1024 * 1024),
    )(starts, record)
    return [flat[slot * homes : (slot + 1) * homes] for slot in range(SLOTS)]


def prepare_kernel(record, rim, *rest):
    pieces = rest[:-4]
    norms, fanned, energy, spread = rest[-4:]
    columns = record.shape[0]
    width = columns + LANES
    sharers = len(pieces)
    sharer = lax.axis_index("panel")
    for source, low, high in ((record, 0, columns), (rim, columns, width)):
        for row in range(low, high, LANES):
            value = source[row - low : row - low + LANES, :].astype(jnp.float32)
            value = value * value
            total = value[:, :LANES]
            for lane in range(LANES, value.shape[1], LANES):
                total = total + value[:, lane : lane + LANES]
            energy[:, row : row + LANES] = lax.dot_general(
                jnp.ones((8, LANES), jnp.float32),
                total,
                (((1,), (1,)), ((), ())),
                precision=lax.Precision.HIGHEST,
                preferred_element_type=jnp.float32,
            )
    value = energy[...]
    stride = 1
    while stride < DELAYS:
        value = value + pltpu.roll(value, stride, 1)
        stride *= 2
    lane = lax.broadcasted_iota(jnp.int32, (8, width), 1)
    value = jnp.where(lane < columns, value, BIG)
    norms[...] = pltpu.roll(value, 0, 1, stride=1, stride_axis=0)
    lane = lax.broadcasted_iota(jnp.int32, (MODES, LANES), 1)
    mode = lax.broadcasted_iota(jnp.int32, (MODES, LANES), 0)
    copies = jnp.where(lax.bitwise_and(lane, MODES - 1) == mode, 1.0, 0.0).astype(jnp.bfloat16)
    rows = columns // sharers
    for hop in range(sharers):
        place = pl.multiple_of(lax.rem(sharer + hop, sharers) * rows, rows)
        spread[pl.ds(place, rows), :] = jnp.dot(pieces[hop][...], copies, preferred_element_type=jnp.float32)
    spread[columns:, :] = jnp.zeros((LANES, LANES), jnp.float32)
    value = spread[...]
    block = lax.broadcasted_iota(jnp.int32, (width, LANES), 1) // MODES
    per = LANES // MODES
    for half in range(2):
        result = jnp.zeros((width, LANES), jnp.float32)
        for part in range(per):
            result = jnp.where(block == part, pltpu.roll(value, half * per + part, 0), result)
        fanned[:, half * LANES : (half + 1) * LANES] = result.astype(jnp.bfloat16)


def prepare(record, rim, pieces):
    width = record.shape[0] + LANES
    vm = pl.BlockSpec(memory_space=pltpu.VMEM)
    return pl.pallas_call(
        prepare_kernel,
        out_shape=[
            jax.ShapeDtypeStruct((8, width), jnp.float32),
            jax.ShapeDtypeStruct((width, 2 * LANES), jnp.bfloat16),
        ],
        in_specs=[vm] * (2 + len(pieces)),
        out_specs=[vm] * 2,
        scratch_shapes=[pltpu.VMEM((8, width), jnp.float32), pltpu.VMEM((width, LANES), jnp.float32)],
        compiler_params=pltpu.CompilerParams(vmem_limit_bytes=40 * 1024 * 1024),
    )(record, rim, *pieces)


def body(record, eigvecs, starts, kernel_width):
    homes = lax.axis_size("tm")
    sharers = lax.axis_size("panel")
    columns, channels = record.shape
    groups = -(-(PANEL + DELAYS - 1 + GROUP - 1) // GROUP)
    deal = -(-groups // homes)
    half = homes // 2
    cut = (deal + 1) // 2 * GROUP
    with jax.named_scope("own_rows"):
        chunks = own_rows(homes, deal, starts, record)
    shards = []
    for slot in range(SLOTS):
        with jax.named_scope("scatter"):
            mine = chunks[slot]
            ahead = step_round(mine[half][:cut], 1)
            back = step_round(mine[half][cut:], -1)
            ahead = mine[half - 1].at[:cut].add(ahead)
            back = mine[half + 1].at[cut:].add(back)
            for hop in range(half - 2, -1, -1):
                ahead = mine[hop] + step_round(ahead, 1)
                back = step_round(back, -1)
                back = back if hop == 0 else mine[homes - hop] + back
            shards.append(ahead + back)
    rim = lax.ppermute(record[columns - LANES :], "tm", [(i, i + 1) for i in range(homes - 1)])
    pieces = [eigvecs]
    for hop in range(1, sharers):
        pieces.append(lax.ppermute(eigvecs, "panel", [((i + hop) % sharers, i) for i in range(sharers)]))
    with jax.named_scope("prepare"):
        norms, fanned = prepare(record, rim, pieces)
        shards, norms, fanned = lax.optimization_barrier((shards, norms, fanned))
    scale = -1.4426950408889634 / (kernel_width * (DELAYS * channels))
    results = []
    with jax.named_scope("gather"):
        for slot in range(SLOTS):
            ahead = back = shards[slot]
            arrived = [(0, 0, ahead)]
            for hop in range(1, half):
                ahead = step_round(ahead, 1)
                back = step_round(back, -1)
                arrived += [(-hop, 0, ahead), (hop, 0, back)]
            arrived.append((half, 0, step_round(ahead[:cut], 1)))
            arrived.append((half, cut, step_round(back[cut:], -1)))
            results.append(arrived)
    with jax.named_scope("panels"):
        partial = panel_call(homes, results, record, rim, fanned, norms, starts, scale)
    total = jnp.sum(lax.all_to_all(partial, "tm", 0, 0), axis=0)
    third = total.shape[0] // SLOTS
    finished = []
    for slot in range(SLOTS):
        own = total[slot * third : (slot + 1) * third]
        rows = jnp.concatenate([own[:, 40 * part : 40 * part + MODES + 1] for part in range(3)], axis=0)
        rows = jnp.flip(rows, axis=0)
        finished.append(rows[:, :MODES] / rows[:, MODES:])
    return jnp.stack(finished)


def solution(mesh):
    placed = (P("tm", None), P(("tm", "panel"), None), P("panel"), P())
    return jax.shard_map(
        body, mesh=mesh, in_specs=placed, out_specs=P("panel", "tm", None), check_vma=False
    )
```

```python
import jax
import jax.numpy as jnp
from jax import lax
from jax.experimental import pallas as pl
from jax.experimental.pallas import tpu as pltpu
from jax.sharding import PartitionSpec as P

DELAYS = 64
PANEL = 768
SLOTS = 2
GROUP = 16
LANES = 128
MODES = 32
BIG = 1e30


def panel_kernel(homes, places, starts, scale, record, rim, vectors, norms, *rest):
    parts = len(places)
    shards = [rest[slot * parts : (slot + 1) * parts] for slot in range(SLOTS)]
    out, window, turned, energies, gram, strips, weights, sums, result = rest[SLOTS * parts :]
    columns = record.shape[0]
    width = columns + LANES
    tiles = width // LANES
    used = turned.shape[1]
    kept = used - DELAYS
    position = ring_position(homes)
    share = PANEL // homes
    third = share // 3
    factor = scale[0]

    def collect(slot):
        for number, (hop, skipped, deal) in enumerate(places):
            chunk = lax.rem(position + (hop % homes), homes)
            shard = shards[slot][number]
            for step in range(0, shard.shape[0], GROUP):
                place = pl.multiple_of(chunk * deal + (skipped + step), GROUP)
                window[pl.ds(place, GROUP), :] = shard[step : step + GROUP, :]
        low = 0
        while low < used:
            count = min(LANES, used - low)
            turn = lax.broadcasted_iota(jnp.int32, (count, count), 0) + lax.broadcasted_iota(jnp.int32, (count, count), 1)
            flip = jnp.where(turn == count - 1, 2.0, 0.0).astype(jnp.bfloat16)
            block = jnp.dot(flip, window[used - low - count : used - low, :], preferred_element_type=jnp.float32)
            turned[slot, low : low + count, :] = block.astype(jnp.bfloat16)
            energy = jnp.sum(block * block, axis=1, keepdims=True) * 0.25
            energies[slot, low : low + count, :] = jnp.broadcast_to(energy, (count, LANES))
            low += count

    def product_with(slot, rows):
        return lax.dot_general(
            turned[slot], rows, (((1,), (1,)), ((), ())), preferred_element_type=jnp.float32
        )

    def turn_rows(slot):
        for row in range(0, used, 8):
            line = pltpu.roll(gram[slot, row : row + 8, :], row % width, 1, stride=1, stride_axis=0)
            for tile in range(tiles):
                strips[tile, row : row + 8, :] = line[:, tile * LANES : (tile + 1) * LANES]

    def add_lags(tile):
        value = strips[tile, :, :]
        stride = 32
        while stride >= 2:
            value = value[stride:] + value[:-stride]
            stride //= 2
        value = value[1:] + value[:-1]
        strips[tile, DELAYS:used, :] = value[1:]

    def weigh(slot):
        for row in range(DELAYS, used, 16):
            halves = []
            for part in range(2):
                at = row + 8 * part
                line = jnp.concatenate([strips[tile, at : at + 8, :] for tile in range(tiles)], axis=1)
                line = pltpu.roll(line, (DELAYS - 1 - at) % width, 1)
                own = jnp.concatenate([strips[tiles, at : at + 8, :]] * tiles, axis=1)
                value = jnp.exp2(((own + norms[...]) - line) * factor)
                total = value[:, :LANES]
                for tile in range(1, tiles):
                    total = total + value[:, tile * LANES : (tile + 1) * LANES]
                sums[at - DELAYS : at - DELAYS + 8, :] = total
                halves.append(value)
            weights[row - DELAYS : row - DELAYS + 16, :] = jnp.concatenate(halves, axis=0).astype(jnp.bfloat16)
        product = jnp.dot(weights[...], vectors[...], preferred_element_type=jnp.float32)
        lane = lax.broadcasted_iota(jnp.int32, (kept, 2 * LANES), 1)
        sub = lax.broadcasted_iota(jnp.int32, (kept, 2 * LANES), 0)
        product = jnp.where(lane // MODES == sub % 8, product, 0.0)
        product = product[:, :LANES] + product[:, LANES:]
        product = product + pltpu.roll(product, 64, 1)
        product = product + pltpu.roll(product, 32, 1)
        lane = lax.broadcasted_iota(jnp.int32, (kept, LANES), 1)
        total = jnp.sum(sums[...], axis=1, keepdims=True)
        product = jnp.where(lane == MODES, total, product)
        result[...] = jnp.where(lane <= MODES, product, 0.0)
        offset = lax.bitwise_and(starts[slot] - (DELAYS - 1), GROUP - 1)
        for home in range(homes):
            start = kept - share * (home + 1) - offset
            packed = result[pl.ds(start, third), :]
            for part in range(1, 3):
                packed = packed + pltpu.roll(result[pl.ds(start + part * third, third), :], 40 * part, 1)
            out[home, slot * third : (slot + 1) * third, :] = packed

    for slot in range(SLOTS):
        collect(slot)
    for slot in range(SLOTS):
        gram[slot, :, :columns] = product_with(slot, record[...])
        gram[slot, :, columns:] = product_with(slot, rim[...])
    for slot in range(SLOTS):
        turn_rows(slot)
        strips[tiles] = energies[slot]
        for tile in range(tiles + 1):
            add_lags(tile)
        weigh(slot)


def panel_call(homes, arrived, record, rim, vectors, norms, starts, scale):
    deal = arrived[0][0][2].shape[0]
    parts = len(arrived[0])
    places = [(hop, skipped, deal) for hop, skipped, _ in arrived[0]]
    shards = [part for slot in range(SLOTS) for _, _, part in arrived[slot]]
    columns = record.shape[0]
    width = columns + LANES
    tiles = width // LANES
    used = -(-(PANEL + DELAYS - 1 + GROUP - 1) // GROUP) * GROUP
    kept = used - DELAYS
    share = PANEL // homes
    vm = pl.BlockSpec(memory_space=pltpu.VMEM)
    sm = pl.BlockSpec(memory_space=pltpu.SMEM)
    return pl.pallas_call(
        lambda *refs: panel_kernel(homes, places, *refs),
        out_shape=jax.ShapeDtypeStruct((homes, SLOTS * (share // 3), LANES), jnp.float32),
        in_specs=[sm, sm] + [vm] * (4 + SLOTS * parts),
        out_specs=vm,
        scratch_shapes=[
            pltpu.VMEM((homes * deal, record.shape[1]), jnp.bfloat16),
            pltpu.VMEM((SLOTS, used, record.shape[1]), jnp.bfloat16),
            pltpu.VMEM((SLOTS, used, LANES), jnp.float32),
            pltpu.VMEM((SLOTS, used, width), jnp.float32),
            pltpu.VMEM((tiles + 1, used, LANES), jnp.float32),
            pltpu.VMEM((kept, width), jnp.bfloat16),
            pltpu.VMEM((kept, LANES), jnp.float32),
            pltpu.VMEM((kept, LANES), jnp.float32),
        ],
        compiler_params=pltpu.CompilerParams(vmem_limit_bytes=46 * 1024 * 1024),
        cost_estimate=pl.CostEstimate(
            flops=2 * SLOTS * used * width * record.shape[1], bytes_accessed=10_000_000, transcendentals=SLOTS * kept * width
        ),
    )(starts, scale, record, rim, vectors, norms, *shards)


def ring_position(homes):
    home = lax.axis_index("tm")
    if homes != 8:
        return home
    return jnp.where(lax.bitwise_and(home, 1) == 0, home, 2 * homes - 1 - home) // 2


def tour(homes):
    if homes != 8:
        return list(range(homes))
    return [0, 2, 4, 6, 7, 5, 3, 1]


def step_round(value, way):
    homes = lax.axis_size("tm")
    order = tour(homes)
    return lax.ppermute(value, "tm", [(order[i], order[(i + way) % homes]) for i in range(homes)])


def first_kernel(homes, deal, cut, starts, record, rim, *rest):
    outs, flags = rest[:-1], rest[-1]
    home = lax.axis_index("tm")
    position = ring_position(homes)
    rows = record.shape[0]
    held = rows // GROUP
    edge = pltpu.make_async_copy(record.at[pl.ds(rows - LANES, LANES)], rim, flags.at[0])
    edge.start()
    waits = []
    for slot in range(SLOTS):
        first = lax.shift_right_arithmetic(starts[slot] - (DELAYS - 1), 4) - home * held
        chunk = lax.rem(position + homes // 2, homes)
        for step in range(deal):
            group = first + chunk * deal + step
            inside = (group >= 0) & (group < held)
            side = 0 if step < cut else 1
            place = (step - cut * side) * GROUP
            target = outs[2 * slot + side].at[pl.ds(place, GROUP)]
            group = lax.clamp(0, group, held - 1)
            source = record.at[pl.ds(pl.multiple_of(group * GROUP, GROUP), GROUP)]
            copy = pltpu.make_async_copy(source, target, flags.at[1 + len(waits)])
            waits.append((inside, copy, target))

            @pl.when(inside)
            def _():
                copy.start()

            @pl.when(jnp.logical_not(inside))
            def _():
                target[...] = jnp.zeros((GROUP, record.shape[1]), record.dtype)

    for inside, copy, _ in waits:

        @pl.when(inside)
        def _():
            copy.wait()

    edge.wait()


def first_rows(homes, deal, cut, starts, record):
    sm = pl.BlockSpec(memory_space=pltpu.SMEM)
    vm = pl.BlockSpec(memory_space=pltpu.VMEM)
    shapes = [jax.ShapeDtypeStruct((LANES, record.shape[1]), record.dtype)]
    for count in (cut, deal - cut) * SLOTS:
        shapes.append(jax.ShapeDtypeStruct((count * GROUP, record.shape[1]), record.dtype))
    return pl.pallas_call(
        lambda *refs: first_kernel(homes, deal, cut, *refs),
        out_shape=shapes,
        in_specs=[sm, pl.BlockSpec(memory_space=pl.ANY)],
        out_specs=[vm] * len(shapes),
        scratch_shapes=[pltpu.SemaphoreType.DMA((1 + SLOTS * deal,))],
        compiler_params=pltpu.CompilerParams(vmem_limit_bytes=60 * 1024 * 1024),
    )(starts, record)


def lane_energy(source, low):
    value = source[low : low + LANES, :].astype(jnp.float32)
    value = value * value
    total = value[:, :LANES]
    for lane in range(LANES, value.shape[1], LANES):
        total = total + value[:, lane : lane + LANES]
    return lax.dot_general(
        jnp.ones((8, LANES), jnp.float32),
        total,
        (((1,), (1,)), ((), ())),
        precision=lax.Precision.HIGHEST,
        preferred_element_type=jnp.float32,
    )


def own_kernel(homes, deal, starts, record, energy, *outs):
    home = lax.axis_index("tm")
    position = ring_position(homes)
    held = record.shape[0] // GROUP
    hops = [hop for hop in range(homes) if hop != homes // 2]
    for slot in range(SLOTS):
        first = lax.shift_right_arithmetic(starts[slot] - (DELAYS - 1), 4) - home * held
        for number, hop in enumerate(hops):
            out = outs[slot * len(hops) + number]
            chunk = lax.rem(position + hop, homes)
            for step in range(deal):
                group = first + chunk * deal + step
                inside = (group >= 0) & (group < held)
                place = slice(step * GROUP, (step + 1) * GROUP)

                @pl.when(inside)
                def _():
                    out[place, :] = record[pl.ds(pl.multiple_of(group * GROUP, GROUP), GROUP), :]

                @pl.when(jnp.logical_not(inside))
                def _():
                    out[place, :] = jnp.zeros((GROUP, out.shape[1]), out.dtype)

    for row in range(0, record.shape[0], LANES):
        energy[:, row : row + LANES] = lane_energy(record, row)


def own_rows(homes, deal, starts, record):
    vm = pl.BlockSpec(memory_space=pltpu.VMEM)
    sm = pl.BlockSpec(memory_space=pltpu.SMEM)
    shape = jax.ShapeDtypeStruct((deal * GROUP, record.shape[1]), record.dtype)
    count = SLOTS * (homes - 1)
    energy, *flat = pl.pallas_call(
        lambda *refs: own_kernel(homes, deal, *refs),
        out_shape=[jax.ShapeDtypeStruct((8, record.shape[0]), jnp.float32)] + [shape] * count,
        in_specs=[sm, vm],
        out_specs=[vm] * (1 + count),
        compiler_params=pltpu.CompilerParams(vmem_limit_bytes=24 * 1024 * 1024),
    )(starts, record)
    chunks = []
    for slot in range(SLOTS):
        part = list(flat[slot * (homes - 1) : (slot + 1) * (homes - 1)])
        part.insert(homes // 2, None)
        chunks.append(part)
    return energy, chunks


def prepare_kernel(energies, rim, *rest):
    pieces = rest[:-4]
    norms, fanned, energy, spread = rest[-4:]
    columns = energies.shape[1]
    width = columns + LANES
    sharers = len(pieces)
    sharer = lax.axis_index("panel")
    energy[:, :columns] = energies[...]
    energy[:, columns:] = lane_energy(rim, 0)
    value = energy[...]
    stride = 1
    while stride < DELAYS:
        value = value + pltpu.roll(value, stride, 1)
        stride *= 2
    lane = lax.broadcasted_iota(jnp.int32, (8, width), 1)
    value = jnp.where(lane < columns, value, BIG)
    norms[...] = pltpu.roll(value, 0, 1, stride=1, stride_axis=0)
    lane = lax.broadcasted_iota(jnp.int32, (MODES, LANES), 1)
    mode = lax.broadcasted_iota(jnp.int32, (MODES, LANES), 0)
    copies = jnp.where(lax.bitwise_and(lane, MODES - 1) == mode, 1.0, 0.0).astype(jnp.bfloat16)
    rows = columns // sharers
    for hop in range(sharers):
        place = pl.multiple_of(lax.rem(sharer + hop, sharers) * rows, rows)
        spread[pl.ds(place, rows), :] = jnp.dot(pieces[hop][...], copies, preferred_element_type=jnp.float32)
    spread[columns:, :] = jnp.zeros((LANES, LANES), jnp.float32)
    value = spread[...]
    block = lax.broadcasted_iota(jnp.int32, (width, LANES), 1) // MODES
    per = LANES // MODES
    for half in range(2):
        result = jnp.zeros((width, LANES), jnp.float32)
        for part in range(per):
            result = jnp.where(block == part, pltpu.roll(value, half * per + part, 0), result)
        fanned[:, half * LANES : (half + 1) * LANES] = result.astype(jnp.bfloat16)


def prepare(energies, rim, pieces):
    width = energies.shape[1] + LANES
    vm = pl.BlockSpec(memory_space=pltpu.VMEM)
    return pl.pallas_call(
        prepare_kernel,
        out_shape=[
            jax.ShapeDtypeStruct((8, width), jnp.float32),
            jax.ShapeDtypeStruct((width, 2 * LANES), jnp.bfloat16),
        ],
        in_specs=[vm] * (2 + len(pieces)),
        out_specs=[vm] * 2,
        scratch_shapes=[pltpu.VMEM((8, width), jnp.float32), pltpu.VMEM((width, LANES), jnp.float32)],
        compiler_params=pltpu.CompilerParams(vmem_limit_bytes=16 * 1024 * 1024),
    )(energies, rim, *pieces)


def body(record, eigvecs, starts, kernel_width):
    homes = lax.axis_size("tm")
    sharers = lax.axis_size("panel")
    columns, channels = record.shape
    groups = -(-(PANEL + DELAYS - 1 + GROUP - 1) // GROUP)
    deal = -(-groups // homes)
    half = homes // 2
    cut = (deal + 1) // 2
    with jax.named_scope("first_rows"):
        rim, *opening = first_rows(homes, deal, cut, starts, record)
    cut = cut * GROUP
    leading = [(step_round(opening[2 * slot], 1), step_round(opening[2 * slot + 1], -1)) for slot in range(SLOTS)]
    eigvecs, leading[1] = lax.optimization_barrier((eigvecs, leading[1]))
    rim, leading[0] = lax.optimization_barrier((rim, leading[0]))
    rim = lax.ppermute(rim, "tm", [(i, i + 1) for i in range(homes - 1)])
    pieces = [eigvecs]
    for hop in range(1, sharers):
        pieces.append(lax.ppermute(eigvecs, "panel", [((i + hop) % sharers, i) for i in range(sharers)]))
    with jax.named_scope("own_rows"):
        energies, chunks = own_rows(homes, deal, starts, record)
    shards = []
    for slot in range(SLOTS):
        with jax.named_scope("scatter"):
            mine = chunks[slot]
            ahead, back = leading[slot]
            ahead = mine[half - 1].at[:cut].add(ahead)
            back = mine[half + 1].at[cut:].add(back)
            for hop in range(half - 2, -1, -1):
                ahead = mine[hop] + step_round(ahead, 1)
                back = step_round(back, -1)
                back = back if hop == 0 else mine[homes - hop] + back
            shards.append(ahead + back)
    energies, shards[0] = lax.optimization_barrier((energies, shards[0]))
    with jax.named_scope("prepare"):
        norms, fanned = prepare(energies, rim, pieces)
    scale = -1.4426950408889634 / (kernel_width * (DELAYS * channels))
    results = []
    with jax.named_scope("gather"):
        for slot in range(SLOTS):
            ahead = back = shards[slot]
            arrived = [(0, 0, ahead)]
            for hop in range(1, half):
                ahead = step_round(ahead, 1)
                back = step_round(back, -1)
                arrived += [(-hop, 0, ahead), (hop, 0, back)]
            arrived.append((half, 0, step_round(ahead[:cut], 1)))
            arrived.append((half, cut, step_round(back[cut:], -1)))
            results.append(arrived)
    with jax.named_scope("panels"):
        partial = panel_call(homes, results, record, rim, fanned, norms, starts, scale)
    total = jnp.sum(lax.all_to_all(partial, "tm", 0, 0), axis=0)
    third = total.shape[0] // SLOTS
    finished = []
    for slot in range(SLOTS):
        own = total[slot * third : (slot + 1) * third]
        rows = jnp.concatenate([own[:, 40 * part : 40 * part + MODES + 1] for part in range(3)], axis=0)
        rows = jnp.flip(rows, axis=0)
        finished.append(rows[:, :MODES] / rows[:, MODES:])
    return jnp.stack(finished)


def solution(mesh):
    placed = (P("tm", None), P(("tm", "panel"), None), P("panel"), P())
    return jax.shard_map(
        body, mesh=mesh, in_specs=placed, out_specs=P("panel", "tm", None), check_vma=False
    )
```
